32 devices in a mesh: dp: 4 (over y, x), seq: 8 (over z, core).
Axes of the slice: x: 2, y: 2, z: 4, core: 2. Of those that a mesh axis runs over, the one named last changes fastest.
Arguments:
- trunk_rows: bfloat16 [4, 4096, 1536], P('dp', 'seq'), may hold values from -6 to 6
- head_grad: bfloat16 [4, 4096, 1536], P('dp', None, 'seq'), may hold values from -6 to 6
- decoder_grad: bfloat16 [4, 8192, 768], P('dp', 'seq'), may hold values from -6 to 6
- pair_grad: bfloat16 [4, 256, 256, 128], P('dp', 'seq'), may hold values from -4 to 4
- conv_weight: bfloat16 [5, 1536, 768], P(None, 'dp'), may hold values from -0.09375 to 0.09375
- left_weight: bfloat16 [1536, 128], replicated, may hold values from -0.625 to 0.625
- right_weight: bfloat16 [1536, 128], replicated, may hold values from -0.625 to 0.625
Outputs:
- grad_rows: bfloat16 [4, 4096, 1536], P('dp', 'seq')
- left_weight_grad: float32 [1536, 128], P('seq')
- right_weight_grad: float32 [1536, 128], P('seq')
The draws below stay inside these ranges and needn't reach their ends.
All inputs are finite; a program needn't handle non-finite values.
Results may differ from the reference program's by a relative error of at most 0.011.
Values may be sent and summed in bfloat16 or wider, within the bound.
A program may use at most 128 MiB of HBM per device.

```python
import jax
import jax.numpy as jnp
from jax import lax

D = 1536
E = 768
C = 128
K = 5
POOL = 16
BATCH = 4
S = 4096
P_SIZE = 256


def steps_of(rng, extent, pieces, smallest, high):
    gain, own = 1.0, jax.random.fold_in(rng, 6)
    for dim, blocks in pieces:
        heights = jnp.exp(jax.random.uniform(jax.random.fold_in(own, dim), (blocks,), jnp.float32, smallest / len(pieces), high / len(pieces)))
        gain = gain * jnp.repeat(heights, extent[dim] // blocks).reshape([-1 if axis == dim else 1 for axis in range(len(extent))])
    return gain


def scatter_about(rng, dims, deviation, reach, split=(), kind=jnp.bfloat16):
    values = jax.random.normal(rng, dims, jnp.float32) * deviation
    if len(split) > 0:
        values = steps_of(rng, dims, split, -0.22, 0.18) * values
    return jnp.clip(values, min=-reach, max=reach).astype(kind)


def setup_inputs(seed: int = 0) -> dict:
    key_of = jax.random.split(jax.random.key(seed), 8)
    trunk_rows = scatter_about(key_of[0], (BATCH, S, D), 1.0, 6.0, ((0, 4), (1, 8)))
    head_grad = scatter_about(key_of[1], (BATCH, S, D), 0.5, 6.0, ((0, 4), (2, 8)))
    decoder_grad = scatter_about(key_of[2], (BATCH, 2 * S, E), 0.5, 6.0, ((0, 4), (1, 8)))
    pair_grad = scatter_about(key_of[3], (BATCH, P_SIZE, P_SIZE, C), 0.25, 4.0, ((0, 4), (1, 8)))
    conv_weight = scatter_about(key_of[4], (K, D, E), (K * E) ** -0.5, 0.09375, ((1, 4),))
    left_weight = scatter_about(key_of[5], (D, C), (D // 16) ** -0.5, 0.625)
    right_weight = scatter_about(key_of[6], (D, C), (D // 16) ** -0.5, 0.625)
    return dict(trunk_rows=trunk_rows, head_grad=head_grad, decoder_grad=decoder_grad, pair_grad=pair_grad, conv_weight=conv_weight, left_weight=left_weight, right_weight=right_weight)


def window_grads(carry, inputs):
    trunk_one, head_one, decoder_one, pair_one, conv_weight, left_weight, right_weight = inputs + carry[2:]
    row_count = trunk_one.shape[0]
    feature_count = trunk_one.shape[1]
    padded = jnp.pad(decoder_one, ((2, 2), (0, 0)))
    spread = jnp.zeros((2 * row_count, feature_count), jnp.float32)
    for offset in range(K):
        spread = spread + jnp.dot(padded[4 - offset:4 - offset + 2 * row_count], conv_weight[offset].T, preferred_element_type=jnp.float32)
    from_decoder = spread.reshape(row_count, 2, feature_count).sum(axis=1)
    pooled = trunk_one.astype(jnp.float32).reshape(row_count // POOL, POOL, feature_count).mean(axis=1).astype(jnp.bfloat16)
    left_proj = jnp.dot(pooled, left_weight, preferred_element_type=jnp.float32).astype(jnp.bfloat16)
    right_proj = jnp.dot(pooled, right_weight, preferred_element_type=jnp.float32).astype(jnp.bfloat16)
    pair_float = pair_one.astype(jnp.float32)
    left_grad = jnp.einsum("ijc,jc->ic", pair_float, right_proj.astype(jnp.float32)).astype(jnp.bfloat16)
    right_grad = jnp.einsum("ijc,ic->jc", pair_float, left_proj.astype(jnp.float32)).astype(jnp.bfloat16)
    pooled_grad = jnp.dot(left_grad, left_weight.T, preferred_element_type=jnp.float32) + jnp.dot(right_grad, right_weight.T, preferred_element_type=jnp.float32)
    from_pair = jnp.repeat(pooled_grad, POOL, axis=0) / POOL
    grad_one = (head_one.astype(jnp.float32) + from_decoder + from_pair).astype(jnp.bfloat16)
    left_sum = carry[0] + jnp.dot(pooled.T, left_grad, preferred_element_type=jnp.float32)
    right_sum = carry[1] + jnp.dot(pooled.T, right_grad, preferred_element_type=jnp.float32)
    return (left_sum, right_sum) + carry[2:], grad_one


def reference(trunk_rows, head_grad, decoder_grad, pair_grad, conv_weight, left_weight, right_weight):
    zeros_grad = jnp.zeros(left_weight.shape, jnp.float32)
    start_carry = (zeros_grad, zeros_grad, conv_weight, left_weight, right_weight)
    final_carry, grad_rows = lax.scan(window_grads, start_carry, (trunk_rows, head_grad, decoder_grad, pair_grad))
    grad_scale = 1.0 / (POOL * BATCH)
    return grad_rows, final_carry[0] * grad_scale, final_carry[1] * grad_scale
```

```python
import functools

import jax
import jax.numpy as jnp
from jax import lax
from jax.experimental import pallas as pl
from jax.experimental.pallas import tpu as pltpu
from jax.sharding import PartitionSpec as P

POOL = 16
MESH = pl.DeviceIdType.MESH
F32 = jnp.float32
BF16 = jnp.bfloat16


def dot_nt(a, b):
    return lax.dot_general(a, b, (((1,), (1,)), ((), ())), preferred_element_type=F32)


def dot_tn(a, b):
    return lax.dot_general(a, b, (((0,), (0,)), ((), ())), preferred_element_type=F32)


def kernel(
    n, ns,
    trunk_hbm, head_hbm, dec_hbm, pair_hbm, conv_hbm, lw_hbm, rw_hbm,
    out_ref, lwg_ref, rwg_ref,
    trunk, lw, rw, pair, dec, wbuf, xbuf, decf, halo,
    hl, hs, hc, hr, acc,
    pooled, pslot, precv, rp_own, rp_all, rpf, lpf, col, crecv, lgf, g_own, g_all, parts, pg,
    loc_sem, hl_sem, hs_send, hs_recv, hr_send, hr_recv, halo_send, halo_recv,
    ex_send, ex_recv, wi_send, wi_recv, ws_send, ws_recv, d_send, d_recv,
):
    d = lax.axis_index("dp")
    me = lax.axis_index("seq")
    nz = ns // 2
    z = me // 2
    c = me % 2
    sib = me + 1 - 2 * c
    rows, feats = trunk.shape
    bins = pooled.shape[0]
    width = head_hbm.shape[1]
    taps, shard, emb = conv_hbm.shape
    half = shard // 2
    ecut = emb // 2
    drows = dec.shape[0]
    chunks = emb // 128

    def remote(src, dst, ssem, rsem, dp, seq):
        return pltpu.make_async_remote_copy(
            src_ref=src, dst_ref=dst, send_sem=ssem, recv_sem=rsem,
            device_id=(dp, seq), device_id_type=MESH,
        )

    barrier = pltpu.get_barrier_semaphore()
    for o in range(1, ns):
        pl.semaphore_signal(barrier, inc=1, device_id=(d, lax.rem(me + o, ns)), device_id_type=MESH)
    for o in range(1, n):
        pl.semaphore_signal(barrier, inc=1, device_id=(lax.rem(d + o, n), me), device_id_type=MESH)

    locals_ = [
        pltpu.make_async_copy(src, dst, loc_sem.at[i])
        for i, (src, dst) in enumerate(
            [(trunk_hbm, trunk), (lw_hbm, lw), (rw_hbm, rw), (pair_hbm, pair), (dec_hbm, dec),
             (conv_hbm, wbuf.at[d])]
        )
    ]
    for copy in locals_:
        copy.start()
    head_local = [
        pltpu.make_async_copy(
            head_hbm.at[pl.ds(pl.multiple_of((2 * t + c) * rows, 16), rows)], hl.at[t], hl_sem.at[t]
        )
        for t in range(nz)
    ]
    for copy in head_local:
        copy.start()
    pl.semaphore_wait(barrier, ns - 1 + n - 1)

    def piece(q):
        return (pl.ds(0, taps), pl.ds(pl.multiple_of(c * half, 16), half), pl.ds(q * ecut, ecut))

    def piece_other(q):
        return (pl.ds(0, taps), pl.ds(pl.multiple_of((1 - c) * half, 16), half), pl.ds(q * ecut, ecut))

    def w_copy(from_hbm, owner, q, dp, slot):
        dst = wbuf.at[(owner,) + piece(q)]
        src = conv_hbm.at[piece(q)] if from_hbm else dst
        return remote(src, dst, wi_send.at[slot], wi_recv.at[owner, q], dp, me)

    def w_wait(owner, q):
        w_copy(False, owner, q, lax.rem(d + 1, n), 0).wait_recv()

    def s_copy(owner, q):
        ref = wbuf.at[(owner,) + piece(q)]
        return remote(ref, ref, ws_send.at[owner, q], ws_recv.at[owner, q], d, sib)

    def s_wait(owner, q):
        ref = wbuf.at[(owner,) + piece_other(q)]
        remote(ref, ref, ws_send.at[owner, q], ws_recv.at[owner, q], d, sib).wait_recv()

    sends = []

    def go(copy):
        copy.start()
        sends.append(copy)

    if n == 4:
        xn = d + 1 - 2 * lax.rem(d, 2)
        yn = lax.rem(d + 2, 4)
        dg = 3 - d
        go(w_copy(True, d, 0, xn, 0))
        go(w_copy(True, d, 1, yn, 1))
        go(w_copy(True, d, 1, xn, 2))
        go(w_copy(True, d, 0, yn, 3))
    else:
        for o in range(1, n):
            for q in range(2):
                go(w_copy(True, d, q, lax.rem(d + o, n), 2 * (o - 1) + q))

    for t in range(nz):
        go(remote(
            head_hbm.at[pl.ds(pl.multiple_of((2 * t + 1 - c) * rows, 16), rows)], hs.at[t],
            hs_send.at[t], hs_recv.at[t], d, sib,
        ))

    up = remote(dec_hbm.at[pl.ds(drows - 16, 16)], halo.at[0], halo_send.at[0], halo_recv.at[0],
                d, lax.rem(me + 1, ns))
    down = remote(dec_hbm.at[pl.ds(0, 16)], halo.at[1], halo_send.at[1], halo_recv.at[1],
                  d, lax.rem(me + ns - 1, ns))
    up.start()
    down.start()

    def exchange(kind, src_of, dst):
        for o in range(1, ns):
            t = lax.rem(me + o, ns)
            go(remote(src_of(t), dst.at[me], ex_send.at[kind, o], ex_recv.at[kind, me], d, t))

    def exchange_wait(kind, dst):
        for o in range(1, ns):
            t = lax.rem(me + o, ns)
            remote(dst.at[t], dst.at[t], ex_send.at[kind, o], ex_recv.at[kind, t], d, t).wait_recv()

    locals_[0].wait()
    locals_[1].wait()
    locals_[2].wait()
    row = lax.broadcasted_iota(jnp.int32, (bins, rows), 1)
    first = lax.broadcasted_iota(jnp.int32, (bins, rows), 0) * POOL
    pool_mat = jnp.where((row >= first) & (row < first + POOL), 1.0 / POOL, 0.0).astype(BF16)
    pooled[...] = jnp.dot(pool_mat, trunk[...], preferred_element_type=F32).astype(BF16)
    right = jnp.dot(pooled[...], rw[...], preferred_element_type=F32).astype(BF16)
    rp_own[...] = right
    rp_all[me] = right
    exchange(0, lambda t: rp_own, rp_all)
    lpf[...] = jnp.dot(pooled[...], lw[...], preferred_element_type=F32).astype(BF16).astype(F32)
    for s in range(ns):
        pslot[s] = pooled[:, s * width:(s + 1) * width]
    precv[me] = pslot[me]

    locals_[3].wait()
    bin_all = pair.shape[1]
    for j in range(bin_all // 128):
        def add_row(i, total):
            return total + pair[i, j * 128:(j + 1) * 128, :].astype(F32) * lpf[pl.ds(i, 1), :]
        total = lax.fori_loop(0, bins, add_row, jnp.zeros((128, 128), F32), unroll=4)
        per = 128 // bins
        for s in range(per):
            col[j * per + s] = total[s * bins:(s + 1) * bins]
    exchange(1, lambda t: col.at[t], crecv)
    crecv[me] = col[me]
    exchange(2, lambda t: pslot.at[t], precv)

    def merge(t, dst, dst_index):
        @pl.when(c == 0)
        def _():
            dst[dst_index] = jnp.concatenate([hl[t], hs[t]], axis=1)

        @pl.when(c == 1)
        def _():
            dst[dst_index] = jnp.concatenate([hs[t], hl[t]], axis=1)

    for t in range(nz):
        head_local[t].wait()
        remote(hs.at[t], hs.at[t], hs_send.at[t], hs_recv.at[t], d, sib).wait_recv()
    for o in range(1, nz):
        t = lax.rem(z + o, nz)
        merge(t, hc, t)
        go(remote(hc.at[t], hr.at[z], hr_send.at[o], hr_recv.at[z], d, 2 * t + c))
    merge(z, hr, z)

    exchange_wait(0, rp_all)
    rpf[...] = rp_all[...].reshape(bin_all, 128).astype(F32)

    def row_sum(i, _):
        lgf[pl.ds(i, 1), :] = jnp.sum(pair[i].astype(F32) * rpf[...], axis=0, keepdims=True)
        return 0

    lax.fori_loop(0, bins, row_sum, 0, unroll=2)
    left_grad = lgf[...].astype(BF16)
    exchange_wait(1, crecv)
    right_sum = crecv[0]
    for s in range(1, ns):
        right_sum = right_sum + crecv[s]
    right_grad = right_sum.astype(BF16)
    g_own[:, 0:128] = left_grad
    g_own[:, 128:256] = right_grad
    g_all[me] = g_own[...]
    exchange(3, lambda t: g_own, g_all)

    locals_[4].wait()
    up.wait()
    down.wait()
    for k in range(chunks):
        lanes = slice(k * 128, (k + 1) * 128)
        decf[k, 0:8] = jnp.where(me > 0, halo[0, 8:16, lanes].astype(F32), 0.0)
        decf[k, 8 + drows:16 + drows] = jnp.where(me < ns - 1, halo[1, 0:8, lanes].astype(F32), 0.0)

        @pl.loop(0, drows // 256)
        def _(b):
            decf[k, pl.ds(pl.multiple_of(8 + b * 256, 8), 256)] = dec[
                pl.ds(pl.multiple_of(b * 256, 256), 256), lanes
            ].astype(F32)

        @pl.loop(0, rows // 128)
        def _(b):
            lines = [decf[k, pl.ds(b * 256 + 8 + o, 128, stride=2), :] for o in range(-2, 4)]
            for tap in range(taps):
                pick = 2 - tap + 2
                xbuf[tap, pl.ds(pl.multiple_of(b * 128, 128), 128), lanes] = (
                    lines[pick] + lines[pick + 1]
                ).astype(BF16)

    def conv(owner):
        @pl.loop(0, rows // 256)
        def _(b):
            block = pl.ds(pl.multiple_of(b * 256, 256), 256)
            total = dot_nt(xbuf[0, block, :], wbuf[owner, 0])
            for tap in range(1, taps):
                total = total + dot_nt(xbuf[tap, block, :], wbuf[owner, tap])
            acc[owner, block, :] = total

    def finish_pair():
        exchange_wait(3, g_all)
        exchange_wait(2, precv)
        part = dot_tn(precv[0], g_all[0])
        for s in range(1, ns):
            part = part + dot_tn(precv[s], g_all[s])
        parts[d] = part.astype(BF16)
        for o in range(1, n):
            go(remote(parts.at[d], parts.at[d], d_send.at[o], d_recv.at[d], lax.rem(d + o, n), me))
        pg[...] = (
            dot_nt(g_own[:, 0:128], lw[...]) + dot_nt(g_own[:, 128:256], rw[...])
        ) * (1.0 / POOL)

    locals_[5].wait()
    if n == 4:
        w_wait(xn, 0)
        go(w_copy(False, xn, 0, yn, 4))
        w_wait(yn, 1)
        go(w_copy(False, yn, 1, xn, 5))
        go(s_copy(xn, 0))
        go(s_copy(yn, 1))
        conv(d)
        finish_pair()
        w_wait(xn, 1)
        go(s_copy(xn, 1))
        w_wait(yn, 0)
        go(s_copy(yn, 0))
        for owner in (xn, yn):
            for q in range(2):
                s_wait(owner, q)
            conv(owner)
        for q in range(2):
            w_wait(dg, q)
            go(s_copy(dg, q))
        for q in range(2):
            s_wait(dg, q)
        conv(dg)
    else:
        conv(d)
        finish_pair()

        def others(o, _):
            owner = lax.rem(d + o, n)
            for q in range(2):
                w_wait(owner, q)
                s_copy(owner, q).start()
            for q in range(2):
                s_wait(owner, q)
            conv(owner)
            for q in range(2):
                s_copy(owner, q).wait_send()
            return 0

        lax.fori_loop(1, n, others, 0)

    for o in range(1, n):
        t = lax.rem(d + o, n)
        remote(parts.at[t], parts.at[t], d_send.at[o], d_recv.at[t], t, me).wait_recv()
    total = parts[0].astype(F32)
    for t in range(1, n):
        total = total + parts[t].astype(F32)
    total = total * (1.0 / (POOL * n))
    lwg_ref[...] = total[:, 0:128]
    rwg_ref[...] = total[:, 128:256]

    for o in range(1, nz):
        t = lax.rem(z + o, nz)
        remote(hr.at[t], hr.at[t], hr_send.at[o], hr_recv.at[t], d, 2 * t + c).wait_recv()

    @pl.loop(0, bins)
    def _(b):
        block = pl.ds(pl.multiple_of(b * POOL, POOL), POOL)
        head = jnp.concatenate([hr[t, block, :].astype(F32) for t in range(nz)], axis=1)
        conv_part = jnp.concatenate([acc[t, block, :] for t in range(n)], axis=1)
        out_ref[block, :] = (head + conv_part + pg[pl.ds(b, 1), :]).astype(BF16)

    for copy in sends:
        copy.wait_send()


def local(n, ns, trunk_rows, head_grad, decoder_grad, pair_grad, conv_weight, left_weight, right_weight):
    rows, feats = trunk_rows.shape[1:]
    width = head_grad.shape[2]
    drows, emb = decoder_grad.shape[1:]
    bins, bin_all, chan = pair_grad.shape[1:]
    taps, shard = conv_weight.shape[:2]
    nz = ns // 2
    dma = pltpu.SemaphoreType.DMA
    out, left, right = pl.pallas_call(
        functools.partial(kernel, n, ns),
        out_shape=(
            jax.ShapeDtypeStruct((rows, feats), BF16),
            jax.ShapeDtypeStruct((width, chan), F32),
            jax.ShapeDtypeStruct((width, chan), F32),
        ),
        in_specs=[pl.BlockSpec(memory_space=pl.ANY)] * 7,
        out_specs=(pl.BlockSpec(memory_space=pltpu.VMEM),) * 3,
        scratch_shapes=[
            pltpu.VMEM((rows, feats), BF16),
            pltpu.VMEM((feats, chan), BF16),
            pltpu.VMEM((feats, chan), BF16),
            pltpu.VMEM((bins, bin_all, chan), BF16),
            pltpu.VMEM((drows, emb), BF16),
            pltpu.VMEM((n, taps, shard, emb), BF16),
            pltpu.VMEM((taps, rows, emb), BF16),
            pltpu.VMEM((emb // 128, drows + 16, 128), F32),
            pltpu.VMEM((2, 16, emb), BF16),
            pltpu.VMEM((nz, rows, width), BF16),
            pltpu.VMEM((nz, rows, width), BF16),
            pltpu.VMEM((nz, rows, 2 * width), BF16),
            pltpu.VMEM((nz, rows, 2 * width), BF16),
            pltpu.VMEM((n, rows, shard), F32),
            pltpu.VMEM((bins, feats), BF16),
            pltpu.VMEM((ns, bins, width), BF16),
            pltpu.VMEM((ns, bins, width), BF16),
            pltpu.VMEM((bins, chan), BF16),
            pltpu.VMEM((ns, bins, chan), BF16),
            pltpu.VMEM((bin_all, chan), F32),
            pltpu.VMEM((bins, chan), F32),
            pltpu.VMEM((ns, bins, chan), F32),
            pltpu.VMEM((ns, bins, chan), F32),
            pltpu.VMEM((bins, chan), F32),
            pltpu.VMEM((bins, 2 * chan), BF16),
            pltpu.VMEM((ns, bins, 2 * chan), BF16),
            pltpu.VMEM((n, width, 2 * chan), BF16),
            pltpu.VMEM((bins, feats), F32),
            dma((6,)), dma((nz,)), dma((nz,)), dma((nz,)), dma((nz,)), dma((nz,)), dma((2,)), dma((2,)),
            dma((4, ns)), dma((4, ns)), dma((2 * n,)), dma((n, 2)), dma((n, 2)), dma((n, 2)),
            dma((n,)), dma((n,)),
        ],
        compiler_params=pltpu.CompilerParams(
            collective_id=0, has_side_effects=True, vmem_limit_bytes=56 * 1024 * 1024
        ),
    )(
        trunk_rows[0], head_grad[0], decoder_grad[0], pair_grad[0], conv_weight, left_weight, right_weight
    )
    return out[None], left, right


def solution(mesh):
    placed = (
        P("dp", "seq", None),
        P("dp", None, "seq"),
        P("dp", "seq", None),
        P("dp", "seq", None, None),
        P(None, "dp", None),
        P(),
        P(),
    )
    return jax.shard_map(
        functools.partial(local, mesh.shape["dp"], mesh.shape["seq"]),
        mesh=mesh,
        in_specs=placed,
        out_specs=(P("dp", "seq", None), P("seq", None), P("seq", None)),
        check_vma=False,
    )
```

```python
import functools

import jax
import jax.numpy as jnp
from jax import lax
from jax.experimental import pallas as pl
from jax.experimental.pallas import tpu as pltpu
from jax.sharding import PartitionSpec as P

POOL = 16
MESH = pl.DeviceIdType.MESH
F32 = jnp.float32
BF16 = jnp.bfloat16


def dot_nt(a, b):
    return lax.dot_general(a, b, (((1,), (1,)), ((), ())), preferred_element_type=F32)


def dot_tn(a, b):
    return lax.dot_general(a, b, (((0,), (0,)), ((), ())), preferred_element_type=F32)


def kernel(
    n, ns,
    trunk_hbm, head_hbm, dec_hbm, pair_hbm, conv_hbm, lw_hbm, rw_hbm,
    out_ref, both_ref,
    trunk, lw, rw, pair, dec, wbuf, xbuf, decf, halo,
    hr, acc,
    pooled, pslot, precv, rp_own, rp_all, rpf, lpf, col, crecv, lgf, g_own, g_all, gx, parts,
    loc_sem, hr_send, hr_recv, halo_send, halo_recv,
    ex_send, ex_recv, wi_send, wi_recv, ws_send, ws_recv, d_send, d_recv,
):
    d = lax.axis_index("dp")
    me = lax.axis_index("seq")
    c = me % 2
    sib = me + 1 - 2 * c
    rows, feats = trunk.shape
    bins = pooled.shape[0]
    width = head_hbm.shape[0]
    taps, shard, emb = conv_hbm.shape
    half = shard // 2
    ecut = emb // 2
    drows = dec.shape[0]
    chunks = emb // 128

    def remote(src, dst, ssem, rsem, dp, seq):
        return pltpu.make_async_remote_copy(
            src_ref=src, dst_ref=dst, send_sem=ssem, recv_sem=rsem,
            device_id=(dp, seq), device_id_type=MESH,
        )

    barrier = pltpu.get_barrier_semaphore()
    for o in range(1, ns):
        pl.semaphore_signal(barrier, inc=1, device_id=(d, lax.rem(me + o, ns)), device_id_type=MESH)
    for o in range(1, n):
        pl.semaphore_signal(barrier, inc=1, device_id=(lax.rem(d + o, n), me), device_id_type=MESH)

    def head_part(t):
        return head_hbm.at[:, pl.ds(pl.multiple_of(t * rows, 128), rows)]

    def feature_rows(t):
        return pl.ds(pl.multiple_of(t * width, 16), width)

    locals_ = [
        pltpu.make_async_copy(src, dst, loc_sem.at[i])
        for i, (src, dst) in enumerate(
            [(trunk_hbm, trunk), (lw_hbm, lw), (rw_hbm, rw), (pair_hbm, pair), (dec_hbm, dec),
             (conv_hbm, wbuf.at[d]), (head_part(me), hr.at[feature_rows(me)])]
        )
    ]
    for copy in locals_:
        copy.start()
    pl.semaphore_wait(barrier, ns - 1 + n - 1)

    def piece(q):
        return (pl.ds(0, taps), pl.ds(pl.multiple_of(c * half, 16), half), pl.ds(q * ecut, ecut))

    def piece_other(q):
        return (pl.ds(0, taps), pl.ds(pl.multiple_of((1 - c) * half, 16), half), pl.ds(q * ecut, ecut))

    def w_copy(from_hbm, owner, q, dp, slot):
        dst = wbuf.at[(owner,) + piece(q)]
        src = conv_hbm.at[piece(q)] if from_hbm else dst
        return remote(src, dst, wi_send.at[slot], wi_recv.at[owner, q], dp, me)

    def w_wait(owner, q):
        w_copy(False, owner, q, lax.rem(d + 1, n), 0).wait_recv()

    def s_copy(owner, q):
        ref = wbuf.at[(owner,) + piece(q)]
        return remote(ref, ref, ws_send.at[owner, q], ws_recv.at[owner, q], d, sib)

    def s_wait(owner, q):
        ref = wbuf.at[(owner,) + piece_other(q)]
        remote(ref, ref, ws_send.at[owner, q], ws_recv.at[owner, q], d, sib).wait_recv()

    sends = []

    def go(copy):
        copy.start()
        sends.append(copy)

    if n == 4:
        xn = d + 1 - 2 * lax.rem(d, 2)
        yn = lax.rem(d + 2, 4)
        dg = 3 - d
        go(w_copy(True, d, 0, xn, 0))
        go(w_copy(True, d, 1, yn, 1))
        go(w_copy(True, d, 1, xn, 2))
        go(w_copy(True, d, 0, yn, 3))
    else:
        for o in range(1, n):
            for q in range(2):
                go(w_copy(True, d, q, lax.rem(d + o, n), 2 * (o - 1) + q))

    def head_copy(o, t, owner):
        return remote(
            head_part(t), hr.at[feature_rows(owner)], hr_send.at[o], hr_recv.at[owner], d, t
        )

    for o in range(1, ns):
        go(head_copy(o, lax.rem(me + o, ns), me))

    up = remote(dec_hbm.at[pl.ds(drows - 16, 16)], halo.at[0], halo_send.at[0], halo_recv.at[0],
                d, lax.rem(me + 1, ns))
    down = remote(dec_hbm.at[pl.ds(0, 16)], halo.at[1], halo_send.at[1], halo_recv.at[1],
                  d, lax.rem(me + ns - 1, ns))
    up.start()
    down.start()

    def exchange(kind, src_of, dst):
        for o in range(1, ns):
            t = lax.rem(me + o, ns)
            go(remote(src_of(t), dst.at[me], ex_send.at[kind, o], ex_recv.at[kind, me], d, t))

    def exchange_wait(kind, dst):
        for o in range(1, ns):
            t = lax.rem(me + o, ns)
            remote(dst.at[t], dst.at[t], ex_send.at[kind, o], ex_recv.at[kind, t], d, t).wait_recv()

    locals_[0].wait()
    locals_[1].wait()
    locals_[2].wait()
    row = lax.broadcasted_iota(jnp.int32, (bins, rows), 1)
    first = lax.broadcasted_iota(jnp.int32, (bins, rows), 0) * POOL
    pool_mat = jnp.where((row >= first) & (row < first + POOL), 1.0 / POOL, 0.0).astype(BF16)
    pooled[...] = jnp.dot(pool_mat, trunk[...], preferred_element_type=F32).astype(BF16)
    right = jnp.dot(pooled[...], rw[...], preferred_element_type=F32).astype(BF16)
    rp_own[...] = right
    rp_all[me] = right
    exchange(0, lambda t: rp_own, rp_all)
    lpf[...] = jnp.dot(pooled[...], lw[...], preferred_element_type=F32).astype(BF16).astype(F32)
    for s in range(ns):
        pslot[s] = pooled[:, s * width:(s + 1) * width]
    precv[me] = pslot[me]

    locals_[3].wait()
    bin_all = pair.shape[1]
    for j in range(bin_all // 128):
        def add_row(i, total):
            return total + pair[i, j * 128:(j + 1) * 128, :].astype(F32) * lpf[pl.ds(i, 1), :]
        total = lax.fori_loop(0, bins, add_row, jnp.zeros((128, 128), F32), unroll=4)
        per = 128 // bins
        for s in range(per):
            col[j * per + s] = total[s * bins:(s + 1) * bins]
    exchange(1, lambda t: col.at[t], crecv)
    crecv[me] = col[me]
    exchange(2, lambda t: pslot.at[t], precv)

    locals_[4].wait()
    up.wait()
    down.wait()
    for k in range(chunks):
        lanes = slice(k * 128, (k + 1) * 128)
        decf[k, 0:8] = jnp.where(me > 0, halo[0, 8:16, lanes].astype(F32), 0.0)
        decf[k, 8 + drows:16 + drows] = jnp.where(me < ns - 1, halo[1, 0:8, lanes].astype(F32), 0.0)

        @pl.loop(0, drows // 256)
        def _(b):
            decf[k, pl.ds(pl.multiple_of(8 + b * 256, 8), 256)] = dec[
                pl.ds(pl.multiple_of(b * 256, 256), 256), lanes
            ].astype(F32)

        @pl.loop(0, rows // 128)
        def _(b):
            lines = [decf[k, pl.ds(b * 256 + 8 + o, 128, stride=2), :] for o in range(-2, 4)]
            for tap in range(taps):
                pick = 2 - tap + 2
                xbuf[tap, pl.ds(pl.multiple_of(b * 128, 128), 128), lanes] = (
                    lines[pick] + lines[pick + 1]
                ).astype(BF16)

    def row_sums():
        exchange_wait(0, rp_all)
        rpf[...] = rp_all[...].reshape(bin_all, 128).astype(F32)

        def row_sum(i, _):
            lgf[pl.ds(i, 1), :] = jnp.sum(pair[i].astype(F32) * rpf[...], axis=0, keepdims=True)
            return 0

        lax.fori_loop(0, bins, row_sum, 0, unroll=2)
        left_grad = lgf[...].astype(BF16)
        exchange_wait(1, crecv)
        right_sum = crecv[0]
        for s in range(1, ns):
            right_sum = right_sum + crecv[s]
        right_grad = right_sum.astype(BF16)
        g_own[:, 0:128] = left_grad
        g_own[:, 128:256] = right_grad
        gx[...] = dot_tn(pool_mat, g_own[...]).astype(BF16)
        g_all[me] = g_own[...]
        exchange(3, lambda t: g_own, g_all)

    unit = (
        lax.broadcasted_iota(jnp.int32, (256, 256), 0) == lax.broadcasted_iota(jnp.int32, (256, 256), 1)
    ).astype(BF16)

    def conv(owner):
        feature = pl.ds(pl.multiple_of(owner * shard, 16), shard)

        @pl.loop(0, rows // 256)
        def _(b):
            block = pl.ds(pl.multiple_of(b * 256, 256), 256)
            total = dot_nt(unit, hr[feature, block])
            total = total + dot_nt(gx[block, 0:128], lw[feature, :])
            total = total + dot_nt(gx[block, 128:256], rw[feature, :])
            for tap in range(taps):
                total = total + dot_nt(xbuf[tap, block, :], wbuf[owner, tap])
            if shard % 128 == 0:
                out_ref[block, pl.ds(pl.multiple_of(owner * shard, 128), shard)] = total.astype(BF16)
            else:
                acc[owner, block, :] = total.astype(BF16)

    def finish_pair():
        exchange_wait(3, g_all)
        exchange_wait(2, precv)
        part = dot_tn(precv[0], g_all[0])
        for s in range(1, ns):
            part = part + dot_tn(precv[s], g_all[s])
        parts[d] = part.astype(BF16)
        for o in range(1, n):
            go(remote(parts.at[d], parts.at[d], d_send.at[o], d_recv.at[d], lax.rem(d + o, n), me))

    def finish_head():
        locals_[5].wait()
        locals_[6].wait()
        for o in range(1, ns):
            t = lax.rem(me + o, ns)
            head_copy(o, t, t).wait_recv()

    if n == 4:
        w_wait(xn, 0)
        go(w_copy(False, xn, 0, yn, 4))
        go(s_copy(xn, 0))
        w_wait(yn, 1)
        go(w_copy(False, yn, 1, xn, 5))
        go(s_copy(yn, 1))
        row_sums()
        w_wait(xn, 1)
        go(s_copy(xn, 1))
        w_wait(yn, 0)
        go(s_copy(yn, 0))
        finish_pair()
        finish_head()
        conv(d)
        for owner in (xn, yn):
            for q in range(2):
                s_wait(owner, q)
            conv(owner)
        for q in range(2):
            w_wait(dg, q)
            go(s_copy(dg, q))
        for q in range(2):
            s_wait(dg, q)
        conv(dg)
    else:
        row_sums()
        finish_pair()
        finish_head()
        conv(d)

        def others(o, _):
            owner = lax.rem(d + o, n)
            for q in range(2):
                w_wait(owner, q)
                s_copy(owner, q).start()
            for q in range(2):
                s_wait(owner, q)
            conv(owner)
            for q in range(2):
                s_copy(owner, q).wait_send()
            return 0

        lax.fori_loop(1, n, others, 0)

    for o in range(1, n):
        t = lax.rem(d + o, n)
        remote(parts.at[t], parts.at[t], d_send.at[o], d_recv.at[t], t, me).wait_recv()
    total = parts[0].astype(F32)
    for t in range(1, n):
        total = total + parts[t].astype(F32)
    both_ref[...] = total * (1.0 / (POOL * n))

    if shard % 128 != 0:
        @pl.loop(0, bins)
        def _(b):
            block = pl.ds(pl.multiple_of(b * POOL, POOL), POOL)
            out_ref[block, :] = jnp.concatenate(
                [acc[t, block, :].astype(F32) for t in range(n)], axis=1
            ).astype(BF16)

    for copy in sends:
        copy.wait_send()


def local(n, ns, trunk_rows, head_grad, decoder_grad, pair_grad, conv_weight, left_weight, right_weight):
    rows, feats = trunk_rows.shape[1:]
    width = head_grad.shape[2]
    drows, emb = decoder_grad.shape[1:]
    bins, bin_all, chan = pair_grad.shape[1:]
    taps, shard = conv_weight.shape[:2]
    spare = (n, rows, shard) if shard % 128 != 0 else (1, 16, 128)
    dma = pltpu.SemaphoreType.DMA
    out, both = pl.pallas_call(
        functools.partial(kernel, n, ns),
        out_shape=(
            jax.ShapeDtypeStruct((rows, feats), BF16),
            jax.ShapeDtypeStruct((width, 2 * chan), F32),
        ),
        in_specs=[pl.BlockSpec(memory_space=pl.ANY)] * 7,
        out_specs=(pl.BlockSpec(memory_space=pltpu.VMEM),) * 2,
        scratch_shapes=[
            pltpu.VMEM((rows, feats), BF16),
            pltpu.VMEM((feats, chan), BF16),
            pltpu.VMEM((feats, chan), BF16),
            pltpu.VMEM((bins, bin_all, chan), BF16),
            pltpu.VMEM((drows, emb), BF16),
            pltpu.VMEM((n, taps, shard, emb), BF16),
            pltpu.VMEM((taps, rows, emb), BF16),
            pltpu.VMEM((emb // 128, drows + 16, 128), F32),
            pltpu.VMEM((2, 16, emb), BF16),
            pltpu.VMEM((feats, rows), BF16),
            pltpu.VMEM(spare, BF16),
            pltpu.VMEM((bins, feats), BF16),
            pltpu.VMEM((ns, bins, width), BF16),
            pltpu.VMEM((ns, bins, width), BF16),
            pltpu.VMEM((bins, chan), BF16),
            pltpu.VMEM((ns, bins, chan), BF16),
            pltpu.VMEM((bin_all, chan), F32),
            pltpu.VMEM((bins, chan), F32),
            pltpu.VMEM((ns, bins, chan), F32),
            pltpu.VMEM((ns, bins, chan), F32),
            pltpu.VMEM((bins, chan), F32),
            pltpu.VMEM((bins, 2 * chan), BF16),
            pltpu.VMEM((ns, bins, 2 * chan), BF16),
            pltpu.VMEM((rows, 2 * chan), BF16),
            pltpu.VMEM((n, width, 2 * chan), BF16),
            dma((7,)), dma((ns,)), dma((ns,)), dma((2,)), dma((2,)),
            dma((4, ns)), dma((4, ns)), dma((2 * n,)), dma((n, 2)), dma((n, 2)), dma((n, 2)),
            dma((n,)), dma((n,)),
        ],
        compiler_params=pltpu.CompilerParams(
            collective_id=0, has_side_effects=True, vmem_limit_bytes=56 * 1024 * 1024
        ),
    )(
        trunk_rows[0], jnp.swapaxes(head_grad[0], 0, 1), decoder_grad[0], pair_grad[0], conv_weight, left_weight, right_weight
    )
    return out[None], both[:, :chan], both[:, chan:]


def solution(mesh):
    placed = (
        P("dp", "seq", None),
        P("dp", None, "seq"),
        P("dp", "seq", None),
        P("dp", "seq", None, None),
        P(None, "dp", None),
        P(),
        P(),
    )
    return jax.shard_map(
        functools.partial(local, mesh.shape["dp"], mesh.shape["seq"]),
        mesh=mesh,
        in_specs=placed,
        out_specs=(P("dp", "seq", None), P("seq", None), P("seq", None)),
        check_vma=False,
    )
```

```python
import functools

import jax
import jax.numpy as jnp
from jax import lax
from jax.experimental import pallas as pl
from jax.experimental.pallas import tpu as pltpu
from jax.sharding import PartitionSpec as P

POOL = 16
MESH = pl.DeviceIdType.MESH
F32 = jnp.float32
BF16 = jnp.bfloat16


def dot_nt(a, b):
    return lax.dot_general(a, b, (((1,), (1,)), ((), ())), preferred_element_type=F32)


def dot_tn(a, b):
    return lax.dot_general(a, b, (((0,), (0,)), ((), ())), preferred_element_type=F32)


def kernel(
    n, ns,
    trunk_hbm, head_hbm, dec_hbm, pair_hbm, conv_hbm, lw_hbm, rw_hbm,
    out_ref, both_ref,
    trunk, lw, rw, pair, dec, wbuf, xbuf, decf, halo,
    hr, acc,
    pooled, pslot, precv, rp_own, rp_all, rpf, lpf, col, crecv, lgf, g_own, g_all, gx, parts,
    loc_sem, hr_send, hr_recv, halo_send, halo_recv,
    ex_send, ex_recv, wi_send, wi_recv, ws_send, ws_recv, d_send, d_recv,
):
    d = lax.axis_index("dp")
    me = lax.axis_index("seq")
    c = me % 2
    sib = me + 1 - 2 * c
    rows, feats = trunk.shape
    bins = pooled.shape[0]
    width = head_hbm.shape[0]
    taps, shard, emb = conv_hbm.shape
    half = shard // 2
    ecut = emb // 2
    drows = dec.shape[0]
    chunks = emb // 128

    def remote(src, dst, ssem, rsem, dp, seq):
        return pltpu.make_async_remote_copy(
            src_ref=src, dst_ref=dst, send_sem=ssem, recv_sem=rsem,
            device_id=(dp, seq), device_id_type=MESH,
        )

    barrier = pltpu.get_barrier_semaphore()
    for o in range(1, ns):
        pl.semaphore_signal(barrier, inc=1, device_id=(d, lax.rem(me + o, ns)), device_id_type=MESH)
    for o in range(1, n):
        pl.semaphore_signal(barrier, inc=1, device_id=(lax.rem(d + o, n), me), device_id_type=MESH)

    def head_part(t):
        return head_hbm.at[:, pl.ds(pl.multiple_of(t * rows, 128), rows)]

    def feature_rows(t):
        return pl.ds(pl.multiple_of(t * width, 16), width)

    locals_ = [
        pltpu.make_async_copy(src, dst, loc_sem.at[i])
        for i, (src, dst) in enumerate(
            [(trunk_hbm, trunk), (lw_hbm, lw), (rw_hbm, rw), (pair_hbm, pair), (dec_hbm, dec),
             (conv_hbm, wbuf.at[d]), (head_part(me), hr.at[feature_rows(me)])]
        )
    ]
    for copy in locals_:
        copy.start()
    pl.semaphore_wait(barrier, ns - 1 + n - 1)

    def piece(q):
        return (pl.ds(0, taps), pl.ds(pl.multiple_of(c * half, 16), half), pl.ds(q * ecut, ecut))

    def piece_other(q):
        return (pl.ds(0, taps), pl.ds(pl.multiple_of((1 - c) * half, 16), half), pl.ds(q * ecut, ecut))

    def w_copy(from_hbm, owner, q, dp, slot):
        dst = wbuf.at[(owner,) + piece(q)]
        src = conv_hbm.at[piece(q)] if from_hbm else dst
        return remote(src, dst, wi_send.at[slot], wi_recv.at[owner, q], dp, me)

    def w_wait(owner, q):
        w_copy(False, owner, q, lax.rem(d + 1, n), 0).wait_recv()

    def s_copy(owner, q):
        ref = wbuf.at[(owner,) + piece(q)]
        return remote(ref, ref, ws_send.at[owner, q], ws_recv.at[owner, q], d, sib)

    def s_wait(owner, q):
        ref = wbuf.at[(owner,) + piece_other(q)]
        remote(ref, ref, ws_send.at[owner, q], ws_recv.at[owner, q], d, sib).wait_recv()

    sends = []

    def go(copy):
        copy.start()
        sends.append(copy)

    if n == 4:
        xn = d + 1 - 2 * lax.rem(d, 2)
        yn = lax.rem(d + 2, 4)
        dg = 3 - d
        go(w_copy(True, d, 0, xn, 0))
        go(w_copy(True, d, 1, yn, 1))
        go(w_copy(True, d, 1, xn, 2))
        go(w_copy(True, d, 0, yn, 3))
    else:
        for o in range(1, n):
            for q in range(2):
                go(w_copy(True, d, q, lax.rem(d + o, n), 2 * (o - 1) + q))

    def head_copy(o, t, owner):
        return remote(
            head_part(t), hr.at[feature_rows(owner)], hr_send.at[o], hr_recv.at[owner], d, t
        )

    for o in sorted(range(1, ns), key=lambda o: abs(2 * o - ns)):
        go(head_copy(o, lax.rem(me + o, ns), me))

    up = remote(dec_hbm.at[pl.ds(drows - 16, 16)], halo.at[0], halo_send.at[0], halo_recv.at[0],
                d, lax.rem(me + 1, ns))
    down = remote(dec_hbm.at[pl.ds(0, 16)], halo.at[1], halo_send.at[1], halo_recv.at[1],
                  d, lax.rem(me + ns - 1, ns))
    up.start()
    down.start()

    def exchange(kind, src_of, dst):
        for o in range(1, ns):
            t = lax.rem(me + o, ns)
            go(remote(src_of(t), dst.at[me], ex_send.at[kind, o], ex_recv.at[kind, me], d, t))

    def exchange_wait(kind, dst):
        for o in range(1, ns):
            t = lax.rem(me + o, ns)
            remote(dst.at[t], dst.at[t], ex_send.at[kind, o], ex_recv.at[kind, t], d, t).wait_recv()

    locals_[0].wait()
    locals_[1].wait()
    locals_[2].wait()
    row = lax.broadcasted_iota(jnp.int32, (bins, rows), 1)
    first = lax.broadcasted_iota(jnp.int32, (bins, rows), 0) * POOL
    pool_mat = jnp.where((row >= first) & (row < first + POOL), 1.0 / POOL, 0.0).astype(BF16)
    pooled[...] = jnp.dot(pool_mat, trunk[...], preferred_element_type=F32).astype(BF16)
    right = jnp.dot(pooled[...], rw[...], preferred_element_type=F32).astype(BF16)
    rp_own[...] = right
    rp_all[me] = right
    exchange(0, lambda t: rp_own, rp_all)
    lpf[...] = jnp.dot(pooled[...], lw[...], preferred_element_type=F32).astype(BF16).astype(F32)
    for s in range(ns):
        pslot[s] = pooled[:, s * width:(s + 1) * width]
    precv[me] = pslot[me]

    locals_[3].wait()
    bin_all = pair.shape[1]
    for j in range(bin_all // 128):
        def add_row(i, total):
            return total + pair[i, j * 128:(j + 1) * 128, :].astype(F32) * lpf[pl.ds(i, 1), :]
        total = lax.fori_loop(0, bins, add_row, jnp.zeros((128, 128), F32), unroll=4)
        per = 128 // bins
        for s in range(per):
            col[j * per + s] = total[s * bins:(s + 1) * bins]
    exchange(1, lambda t: col.at[t], crecv)
    crecv[me] = col[me]
    exchange(2, lambda t: pslot.at[t], precv)

    locals_[4].wait()
    up.wait()
    down.wait()
    for k in range(chunks):
        lanes = slice(k * 128, (k + 1) * 128)
        decf[k, 0:8] = jnp.where(me > 0, halo[0, 8:16, lanes].astype(F32), 0.0)
        decf[k, 8 + drows:16 + drows] = jnp.where(me < ns - 1, halo[1, 0:8, lanes].astype(F32), 0.0)

        @pl.loop(0, drows // 256)
        def _(b):
            decf[k, pl.ds(pl.multiple_of(8 + b * 256, 8), 256)] = dec[
                pl.ds(pl.multiple_of(b * 256, 256), 256), lanes
            ].astype(F32)

        @pl.loop(0, rows // 128)
        def _(b):
            lines = [decf[k, pl.ds(b * 256 + 8 + o, 128, stride=2), :] for o in range(-2, 4)]
            for tap in range(taps):
                pick = 2 - tap + 2
                xbuf[tap, pl.ds(pl.multiple_of(b * 128, 128), 128), lanes] = (
                    lines[pick] + lines[pick + 1]
                ).astype(BF16)

    def row_sums():
        exchange_wait(0, rp_all)
        rpf[...] = rp_all[...].reshape(bin_all, 128).astype(F32)

        def row_sum(i, _):
            lgf[pl.ds(i, 1), :] = jnp.sum(pair[i].astype(F32) * rpf[...], axis=0, keepdims=True)
            return 0

        lax.fori_loop(0, bins, row_sum, 0, unroll=2)
        left_grad = lgf[...].astype(BF16)
        exchange_wait(1, crecv)
        right_sum = crecv[0]
        for s in range(1, ns):
            right_sum = right_sum + crecv[s]
        right_grad = right_sum.astype(BF16)
        g_own[:, 0:128] = left_grad
        g_own[:, 128:256] = right_grad
        gx[...] = dot_tn(pool_mat, g_own[...]).astype(BF16)
        g_all[me] = g_own[...]
        exchange(3, lambda t: g_own, g_all)

    unit = (
        lax.broadcasted_iota(jnp.int32, (256, 256), 0) == lax.broadcasted_iota(jnp.int32, (256, 256), 1)
    ).astype(BF16)

    def conv(owner):
        @pl.loop(0, rows // 256)
        def _(b):
            block = pl.ds(pl.multiple_of(b * 256, 256), 256)
            total = dot_nt(xbuf[0, block, :], wbuf[owner, 0])
            for tap in range(1, taps):
                total = total + dot_nt(xbuf[tap, block, :], wbuf[owner, tap])
            acc[owner, block, :] = total

    def finish(owner):
        feature = pl.ds(pl.multiple_of(owner * shard, 16), shard)

        @pl.loop(0, rows // 256)
        def _(b):
            block = pl.ds(pl.multiple_of(b * 256, 256), 256)
            total = acc[owner, block, :] + dot_nt(unit, hr[feature, block])
            total = total + dot_nt(gx[block, 0:128], lw[feature, :])
            total = total + dot_nt(gx[block, 128:256], rw[feature, :])
            if shard % 128 == 0:
                out_ref[block, pl.ds(pl.multiple_of(owner * shard, 128), shard)] = total.astype(BF16)
            else:
                acc[owner, block, :] = total

    def finish_pair():
        exchange_wait(3, g_all)
        exchange_wait(2, precv)
        part = dot_tn(precv[0], g_all[0])
        for s in range(1, ns):
            part = part + dot_tn(precv[s], g_all[s])
        parts[d] = part.astype(BF16)
        for o in range(1, n):
            go(remote(parts.at[d], parts.at[d], d_send.at[o], d_recv.at[d], lax.rem(d + o, n), me))

    def finish_head():
        locals_[6].wait()
        for o in range(1, ns):
            t = lax.rem(me + o, ns)
            head_copy(o, t, t).wait_recv()

    if n == 4:
        w_wait(xn, 0)
        go(w_copy(False, xn, 0, yn, 4))
        go(s_copy(xn, 0))
        w_wait(yn, 1)
        go(w_copy(False, yn, 1, xn, 5))
        go(s_copy(yn, 1))
        row_sums()
        locals_[5].wait()
        conv(d)
        w_wait(xn, 1)
        go(s_copy(xn, 1))
        w_wait(yn, 0)
        go(s_copy(yn, 0))
        finish_pair()
        for owner in (xn, yn):
            for q in range(2):
                s_wait(owner, q)
            conv(owner)
        for q in range(2):
            w_wait(dg, q)
            go(s_copy(dg, q))
        for q in range(2):
            s_wait(dg, q)
        conv(dg)
    else:
        row_sums()
        finish_pair()
        locals_[5].wait()
        conv(d)

        def others(o, _):
            owner = lax.rem(d + o, n)
            for q in range(2):
                w_wait(owner, q)
                s_copy(owner, q).start()
            for q in range(2):
                s_wait(owner, q)
            conv(owner)
            for q in range(2):
                s_copy(owner, q).wait_send()
            return 0

        lax.fori_loop(1, n, others, 0)

    for o in range(1, n):
        t = lax.rem(d + o, n)
        remote(parts.at[t], parts.at[t], d_send.at[o], d_recv.at[t], t, me).wait_recv()
    total = parts[0].astype(F32)
    for t in range(1, n):
        total = total + parts[t].astype(F32)
    both_ref[...] = total * (1.0 / (POOL * n))

    finish_head()

    @pl.loop(0, n)
    def _(owner):
        finish(owner)

    if shard % 128 != 0:
        @pl.loop(0, bins)
        def _(b):
            block = pl.ds(pl.multiple_of(b * POOL, POOL), POOL)
            out_ref[block, :] = jnp.concatenate(
                [acc[t, block, :] for t in range(n)], axis=1
            ).astype(BF16)

    for copy in sends:
        copy.wait_send()


def local(n, ns, trunk_rows, head_grad, decoder_grad, pair_grad, conv_weight, left_weight, right_weight):
    rows, feats = trunk_rows.shape[1:]
    width = head_grad.shape[2]
    drows, emb = decoder_grad.shape[1:]
    bins, bin_all, chan = pair_grad.shape[1:]
    taps, shard = conv_weight.shape[:2]
    dma = pltpu.SemaphoreType.DMA
    out, both = pl.pallas_call(
        functools.partial(kernel, n, ns),
        out_shape=(
            jax.ShapeDtypeStruct((rows, feats), BF16),
            jax.ShapeDtypeStruct((width, 2 * chan), F32),
        ),
        in_specs=[pl.BlockSpec(memory_space=pl.ANY)] * 7,
        out_specs=(pl.BlockSpec(memory_space=pltpu.VMEM),) * 2,
        scratch_shapes=[
            pltpu.VMEM((rows, feats), BF16),
            pltpu.VMEM((feats, chan), BF16),
            pltpu.VMEM((feats, chan), BF16),
            pltpu.VMEM((bins, bin_all, chan), BF16),
            pltpu.VMEM((drows, emb), BF16),
            pltpu.VMEM((n, taps, shard, emb), BF16),
            pltpu.VMEM((taps, rows, emb), BF16),
            pltpu.VMEM((emb // 128, drows + 16, 128), F32),
            pltpu.VMEM((2, 16, emb), BF16),
            pltpu.VMEM((feats, rows), BF16),
            pltpu.VMEM((n, rows, shard), F32),
            pltpu.VMEM((bins, feats), BF16),
            pltpu.VMEM((ns, bins, width), BF16),
            pltpu.VMEM((ns, bins, width), BF16),
            pltpu.VMEM((bins, chan), BF16),
            pltpu.VMEM((ns, bins, chan), BF16),
            pltpu.VMEM((bin_all, chan), F32),
            pltpu.VMEM((bins, chan), F32),
            pltpu.VMEM((ns, bins, chan), F32),
            pltpu.VMEM((ns, bins, chan), F32),
            pltpu.VMEM((bins, chan), F32),
            pltpu.VMEM((bins, 2 * chan), BF16),
            pltpu.VMEM((ns, bins, 2 * chan), BF16),
            pltpu.VMEM((rows, 2 * chan), BF16),
            pltpu.VMEM((n, width, 2 * chan), BF16),
            dma((7,)), dma((ns,)), dma((ns,)), dma((2,)), dma((2,)),
            dma((4, ns)), dma((4, ns)), dma((2 * n,)), dma((n, 2)), dma((n, 2)), dma((n, 2)),
            dma((n,)), dma((n,)),
        ],
        compiler_params=pltpu.CompilerParams(
            collective_id=0, has_side_effects=True, vmem_limit_bytes=56 * 1024 * 1024
        ),
    )(
        trunk_rows[0], jnp.swapaxes(head_grad[0], 0, 1), decoder_grad[0], pair_grad[0], conv_weight, left_weight, right_weight
    )
    return out[None], both[:, :chan], both[:, chan:]


def solution(mesh):
    placed = (
        P("dp", "seq", None),
        P("dp", None, "seq"),
        P("dp", "seq", None),
        P("dp", "seq", None, None),
        P(None, "dp", None),
        P(),
        P(),
    )
    return jax.shard_map(
        functools.partial(local, mesh.shape["dp"], mesh.shape["seq"]),
        mesh=mesh,
        in_specs=placed,
        out_specs=(P("dp", "seq", None), P("seq", None), P("seq", None)),
        check_vma=False,
    )
```

```python
import functools

import jax
import jax.numpy as jnp
from jax import lax
from jax.experimental import pallas as pl
from jax.experimental.pallas import tpu as pltpu
from jax.sharding import PartitionSpec as P

POOL = 16
MESH = pl.DeviceIdType.MESH
F32 = jnp.float32
BF16 = jnp.bfloat16


def dot_nt(a, b):
    return lax.dot_general(a, b, (((1,), (1,)), ((), ())), preferred_element_type=F32)


def dot_tn(a, b):
    return lax.dot_general(a, b, (((0,), (0,)), ((), ())), preferred_element_type=F32)


def kernel(
    n, ns,
    trunk_hbm, head_hbm, dec_hbm, pair_hbm, conv_hbm, lw_hbm, rw_hbm,
    out_ref, both_ref,
    trunk, lw, rw, pair, dec, wbuf, xbuf, decf, halo,
    hr, acc,
    pooled, pslot, precv, rp_own, rp_all, rpf, lpf, col, crecv, lgf, g_own, g_all, gx, parts,
    loc_sem, hr_send, hr_recv, halo_send, halo_recv,
    ex_send, ex_recv, wi_send, wi_recv, ws_send, ws_recv, d_send, d_recv,
):
    d = lax.axis_index("dp")
    me = lax.axis_index("seq")
    c = me % 2
    sib = me + 1 - 2 * c
    rows, feats = trunk.shape
    bins = pooled.shape[0]
    width = head_hbm.shape[0]
    taps, shard, emb = conv_hbm.shape
    half = shard // 2
    ecut = emb // 2
    drows = dec.shape[0]
    chunks = emb // 128

    def remote(src, dst, ssem, rsem, dp, seq):
        return pltpu.make_async_remote_copy(
            src_ref=src, dst_ref=dst, send_sem=ssem, recv_sem=rsem,
            device_id=(dp, seq), device_id_type=MESH,
        )

    barrier = pltpu.get_barrier_semaphore()
    for o in range(1, ns):
        pl.semaphore_signal(barrier, inc=1, device_id=(d, lax.rem(me + o, ns)), device_id_type=MESH)
    for o in range(1, n):
        pl.semaphore_signal(barrier, inc=1, device_id=(lax.rem(d + o, n), me), device_id_type=MESH)

    def head_part(t):
        return head_hbm.at[:, pl.ds(pl.multiple_of(t * rows, 128), rows)]

    def feature_rows(t):
        return pl.ds(pl.multiple_of(t * width, 16), width)

    locals_ = [
        pltpu.make_async_copy(src, dst, loc_sem.at[i])
        for i, (src, dst) in enumerate(
            [(trunk_hbm, trunk), (lw_hbm, lw), (rw_hbm, rw), (pair_hbm, pair), (dec_hbm, dec),
             (conv_hbm, wbuf.at[d]), (head_part(me), hr.at[feature_rows(me)])]
        )
    ]
    for copy in locals_:
        copy.start()
    pl.semaphore_wait(barrier, ns - 1 + n - 1)

    def piece(q):
        return (pl.ds(0, taps), pl.ds(pl.multiple_of(c * half, 16), half), pl.ds(q * ecut, ecut))

    def piece_other(q):
        return (pl.ds(0, taps), pl.ds(pl.multiple_of((1 - c) * half, 16), half), pl.ds(q * ecut, ecut))

    def w_copy(from_hbm, owner, q, dp, slot):
        dst = wbuf.at[(owner,) + piece(q)]
        src = conv_hbm.at[piece(q)] if from_hbm else dst
        return remote(src, dst, wi_send.at[slot], wi_recv.at[owner, q], dp, me)

    def w_wait(owner, q):
        w_copy(False, owner, q, lax.rem(d + 1, n), 0).wait_recv()

    def s_copy(owner, q):
        ref = wbuf.at[(owner,) + piece(q)]
        return remote(ref, ref, ws_send.at[owner, q], ws_recv.at[owner, q], d, sib)

    def s_wait(owner, q):
        ref = wbuf.at[(owner,) + piece_other(q)]
        remote(ref, ref, ws_send.at[owner, q], ws_recv.at[owner, q], d, sib).wait_recv()

    sends = []

    def go(copy):
        copy.start()
        sends.append(copy)

    if n == 4:
        xn = d + 1 - 2 * lax.rem(d, 2)
        yn = lax.rem(d + 2, 4)
        dg = 3 - d
        go(w_copy(True, d, 0, xn, 0))
        go(w_copy(True, d, 1, yn, 1))
        go(w_copy(True, d, 1, xn, 2))
        go(w_copy(True, d, 0, yn, 3))
    else:
        for o in range(1, n):
            for q in range(2):
                go(w_copy(True, d, q, lax.rem(d + o, n), 2 * (o - 1) + q))

    up = remote(dec_hbm.at[pl.ds(drows - 16, 16)], halo.at[0], halo_send.at[0], halo_recv.at[0],
                d, lax.rem(me + 1, ns))
    down = remote(dec_hbm.at[pl.ds(0, 16)], halo.at[1], halo_send.at[1], halo_recv.at[1],
                  d, lax.rem(me + ns - 1, ns))
    up.start()
    down.start()

    def head_copy(o, t, owner):
        return remote(
            head_part(t), hr.at[feature_rows(owner)], hr_send.at[o], hr_recv.at[owner], d, t
        )

    for o in sorted(range(1, ns), key=lambda o: abs(2 * o - ns)):
        go(head_copy(o, lax.rem(me + o, ns), me))

    def exchange(kind, src_of, dst):
        for o in range(1, ns):
            t = lax.rem(me + o, ns)
            go(remote(src_of(t), dst.at[me], ex_send.at[kind, o], ex_recv.at[kind, me], d, t))

    def exchange_wait(kind, dst):
        for o in range(1, ns):
            t = lax.rem(me + o, ns)
            remote(dst.at[t], dst.at[t], ex_send.at[kind, o], ex_recv.at[kind, t], d, t).wait_recv()

    locals_[0].wait()
    locals_[1].wait()
    locals_[2].wait()
    row = lax.broadcasted_iota(jnp.int32, (bins, rows), 1)
    first = lax.broadcasted_iota(jnp.int32, (bins, rows), 0) * POOL
    pool_mat = jnp.where((row >= first) & (row < first + POOL), 1.0 / POOL, 0.0).astype(BF16)
    pooled[...] = jnp.dot(pool_mat, trunk[...], preferred_element_type=F32).astype(BF16)
    right = jnp.dot(pooled[...], rw[...], preferred_element_type=F32).astype(BF16)
    rp_own[...] = right
    rp_all[me] = right
    exchange(0, lambda t: rp_own, rp_all)
    lpf[...] = jnp.dot(pooled[...], lw[...], preferred_element_type=F32).astype(BF16).astype(F32)
    for s in range(ns):
        pslot[s] = pooled[:, s * width:(s + 1) * width]
    precv[me] = pslot[me]

    locals_[3].wait()
    bin_all = pair.shape[1]
    for j in range(bin_all // 128):
        def add_row(i, total):
            return total + pair[i, j * 128:(j + 1) * 128, :].astype(F32) * lpf[pl.ds(i, 1), :]
        total = lax.fori_loop(0, bins, add_row, jnp.zeros((128, 128), F32), unroll=4)
        per = 128 // bins
        for s in range(per):
            col[j * per + s] = total[s * bins:(s + 1) * bins]
    exchange(1, lambda t: col.at[t], crecv)
    crecv[me] = col[me]
    exchange(2, lambda t: pslot.at[t], precv)

    locals_[4].wait()
    up.wait()
    down.wait()
    for k in range(chunks):
        lanes = slice(k * 128, (k + 1) * 128)
        decf[k, 0:8] = jnp.where(me > 0, halo[0, 8:16, lanes].astype(F32), 0.0)
        decf[k, 8 + drows:16 + drows] = jnp.where(me < ns - 1, halo[1, 0:8, lanes].astype(F32), 0.0)

        @pl.loop(0, drows // 256)
        def _(b):
            decf[k, pl.ds(pl.multiple_of(8 + b * 256, 8), 256)] = dec[
                pl.ds(pl.multiple_of(b * 256, 256), 256), lanes
            ].astype(F32)

        @pl.loop(0, rows // 128)
        def _(b):
            lines = [decf[k, pl.ds(b * 256 + 8 + o, 128, stride=2), :] for o in range(-2, 4)]
            for tap in range(taps):
                pick = 2 - tap + 2
                xbuf[tap, pl.ds(pl.multiple_of(b * 128, 128), 128), lanes] = (
                    lines[pick] + lines[pick + 1]
                ).astype(BF16)

    def row_sums():
        exchange_wait(0, rp_all)
        rpf[...] = rp_all[...].reshape(bin_all, 128).astype(F32)

        def row_sum(i, _):
            lgf[pl.ds(i, 1), :] = jnp.sum(pair[i].astype(F32) * rpf[...], axis=0, keepdims=True)
            return 0

        lax.fori_loop(0, bins, row_sum, 0, unroll=2)
        left_grad = lgf[...].astype(BF16)
        exchange_wait(1, crecv)
        right_sum = crecv[0]
        for s in range(1, ns):
            right_sum = right_sum + crecv[s]
        right_grad = right_sum.astype(BF16)
        g_own[:, 0:128] = left_grad
        g_own[:, 128:256] = right_grad
        gx[...] = dot_tn(pool_mat, g_own[...]).astype(BF16)
        g_all[me] = g_own[...]
        exchange(3, lambda t: g_own, g_all)

    unit = (
        lax.broadcasted_iota(jnp.int32, (256, 256), 0) == lax.broadcasted_iota(jnp.int32, (256, 256), 1)
    ).astype(BF16)

    def conv(owner):
        @pl.loop(0, rows // 256)
        def _(b):
            block = pl.ds(pl.multiple_of(b * 256, 256), 256)
            total = dot_nt(xbuf[0, block, :], wbuf[owner, 0])
            for tap in range(1, taps):
                total = total + dot_nt(xbuf[tap, block, :], wbuf[owner, tap])
            acc[owner, block, :] = total

    def finish(owner):
        feature = pl.ds(pl.multiple_of(owner * shard, 16), shard)

        @pl.loop(0, rows // 256)
        def _(b):
            block = pl.ds(pl.multiple_of(b * 256, 256), 256)
            total = acc[owner, block, :] + dot_nt(unit, hr[feature, block])
            total = total + dot_nt(gx[block, 0:128], lw[feature, :])
            total = total + dot_nt(gx[block, 128:256], rw[feature, :])
            if shard % 128 == 0:
                out_ref[block, pl.ds(pl.multiple_of(owner * shard, 128), shard)] = total.astype(BF16)
            else:
                acc[owner, block, :] = total

    def finish_pair():
        exchange_wait(3, g_all)
        exchange_wait(2, precv)
        part = dot_tn(precv[0], g_all[0])
        for s in range(1, ns):
            part = part + dot_tn(precv[s], g_all[s])
        parts[d] = part.astype(BF16)
        for o in range(1, n):
            go(remote(parts.at[d], parts.at[d], d_send.at[o], d_recv.at[d], lax.rem(d + o, n), me))

    def finish_head():
        locals_[6].wait()
        for o in range(1, ns):
            t = lax.rem(me + o, ns)
            head_copy(o, t, t).wait_recv()

    if n == 4:
        w_wait(xn, 0)
        go(w_copy(False, xn, 0, yn, 4))
        go(s_copy(xn, 0))
        w_wait(yn, 1)
        go(w_copy(False, yn, 1, xn, 5))
        go(s_copy(yn, 1))
        row_sums()
        locals_[5].wait()
        conv(d)
        w_wait(xn, 1)
        go(s_copy(xn, 1))
        w_wait(yn, 0)
        go(s_copy(yn, 0))
        finish_pair()
        for owner in (xn, yn):
            for q in range(2):
                s_wait(owner, q)
            conv(owner)
        for q in range(2):
            w_wait(dg, q)
            go(s_copy(dg, q))
        for q in range(2):
            s_wait(dg, q)
        conv(dg)
    else:
        row_sums()
        finish_pair()
        locals_[5].wait()
        conv(d)

        def others(o, _):
            owner = lax.rem(d + o, n)
            for q in range(2):
                w_wait(owner, q)
                s_copy(owner, q).start()
            for q in range(2):
                s_wait(owner, q)
            conv(owner)
            for q in range(2):
                s_copy(owner, q).wait_send()
            return 0

        lax.fori_loop(1, n, others, 0)

    for o in range(1, n):
        t = lax.rem(d + o, n)
        remote(parts.at[t], parts.at[t], d_send.at[o], d_recv.at[t], t, me).wait_recv()
    total = parts[0].astype(F32)
    for t in range(1, n):
        total = total + parts[t].astype(F32)
    both_ref[...] = total * (1.0 / (POOL * n))

    finish_head()

    @pl.loop(0, n)
    def _(owner):
        finish(owner)

    if shard % 128 != 0:
        @pl.loop(0, bins)
        def _(b):
            block = pl.ds(pl.multiple_of(b * POOL, POOL), POOL)
            out_ref[block, :] = jnp.concatenate(
                [acc[t, block, :] for t in range(n)], axis=1
            ).astype(BF16)

    for copy in sends:
        copy.wait_send()


def local(n, ns, trunk_rows, head_grad, decoder_grad, pair_grad, conv_weight, left_weight, right_weight):
    rows, feats = trunk_rows.shape[1:]
    width = head_grad.shape[2]
    drows, emb = decoder_grad.shape[1:]
    bins, bin_all, chan = pair_grad.shape[1:]
    taps, shard = conv_weight.shape[:2]
    dma = pltpu.SemaphoreType.DMA
    out, both = pl.pallas_call(
        functools.partial(kernel, n, ns),
        out_shape=(
            jax.ShapeDtypeStruct((rows, feats), BF16),
            jax.ShapeDtypeStruct((width, 2 * chan), F32),
        ),
        in_specs=[pl.BlockSpec(memory_space=pl.ANY)] * 7,
        out_specs=(pl.BlockSpec(memory_space=pltpu.VMEM),) * 2,
        scratch_shapes=[
            pltpu.VMEM((rows, feats), BF16),
            pltpu.VMEM((feats, chan), BF16),
            pltpu.VMEM((feats, chan), BF16),
            pltpu.VMEM((bins, bin_all, chan), BF16),
            pltpu.VMEM((drows, emb), BF16),
            pltpu.VMEM((n, taps, shard, emb), BF16),
            pltpu.VMEM((taps, rows, emb), BF16),
            pltpu.VMEM((emb // 128, drows + 16, 128), F32),
            pltpu.VMEM((2, 16, emb), BF16),
            pltpu.VMEM((feats, rows), BF16),
            pltpu.VMEM((n, rows, shard), F32),
            pltpu.VMEM((bins, feats), BF16),
            pltpu.VMEM((ns, bins, width), BF16),
            pltpu.VMEM((ns, bins, width), BF16),
            pltpu.VMEM((bins, chan), BF16),
            pltpu.VMEM((ns, bins, chan), BF16),
            pltpu.VMEM((bin_all, chan), F32),
            pltpu.VMEM((bins, chan), F32),
            pltpu.VMEM((ns, bins, chan), F32),
            pltpu.VMEM((ns, bins, chan), F32),
            pltpu.VMEM((bins, chan), F32),
            pltpu.VMEM((bins, 2 * chan), BF16),
            pltpu.VMEM((ns, bins, 2 * chan), BF16),
            pltpu.VMEM((rows, 2 * chan), BF16),
            pltpu.VMEM((n, width, 2 * chan), BF16),
            dma((7,)), dma((ns,)), dma((ns,)), dma((2,)), dma((2,)),
            dma((4, ns)), dma((4, ns)), dma((2 * n,)), dma((n, 2)), dma((n, 2)), dma((n, 2)),
            dma((n,)), dma((n,)),
        ],
        compiler_params=pltpu.CompilerParams(
            collective_id=0, has_side_effects=True, vmem_limit_bytes=56 * 1024 * 1024
        ),
    )(
        trunk_rows[0], jnp.swapaxes(head_grad[0], 0, 1), decoder_grad[0], pair_grad[0], conv_weight, left_weight, right_weight
    )
    return out[None], both[:, :chan], both[:, chan:]


def solution(mesh):
    placed = (
        P("dp", "seq", None),
        P("dp", None, "seq"),
        P("dp", "seq", None),
        P("dp", "seq", None, None),
        P(None, "dp", None),
        P(),
        P(),
    )
    return jax.shard_map(
        functools.partial(local, mesh.shape["dp"], mesh.shape["seq"]),
        mesh=mesh,
        in_specs=placed,
        out_specs=(P("dp", "seq", None), P("seq", None), P("seq", None)),
        check_vma=False,
    )
```
